256 devices in a mesh: snp: 4 (over x), rows: 64 (over y, z, core).
Axes of the slice: x: 4, y: 4, z: 8, core: 2. Of those that a mesh axis runs over, the one named last changes fastest.
Arguments:
- genotypes: float32 [3072, 10240], P('snp', 'rows'), may hold values from -1 to 2, as said below
- relationship: float32 [10240, 10240], P('rows', 'snp'), as said below
Outputs:
- updated: float32 [10240, 10240], P('rows', 'snp')
- panel: float32 [10240, 512], P('rows')
The draws below stay inside these ranges and needn't reach their ends.
Inputs may be any that keep to these rules, and one draw needn't show every extreme that they name: `genotypes`: expected count of the alternative allele, a real number between 0 and 2; exactly -1 marks a missing call. `relationship`: symmetric.
All inputs are finite; a program needn't handle non-finite values.
Results may differ from the reference program's by a relative error of at most 0.0007.
The reference program's roundings to bfloat16 on the way (of `centered`) count: a program that leaves them out, or rounds other values in their place, can miss the bound.
Values may be sent and summed in bfloat16 or wider, within the bound.
A program may use at most 128 MiB of HBM per device.

```python
import math
import jax
import jax.numpy as jnp
from jax import lax

SNPS = 3072
PANEL = 512
INDIV = 10240


def draw_genotypes(key, part):
    key = jax.random.fold_in(key, 11)
    key_freq, key_first, key_second, key_noise_one, key_noise_two, key_missing = jax.random.split(key, 6)
    percent = jax.random.randint(key_freq, (SNPS, 1), 5, 51)
    first_allele = jax.random.randint(key_first, (SNPS, INDIV), 0, 100) < percent
    second_allele = jax.random.randint(key_second, (SNPS, INDIV), 0, 100) < percent
    missing = jax.random.randint(key_missing, (SNPS, INDIV), 0, 50) == 0
    noise_one = jax.random.normal(key_noise_one, (SNPS, INDIV), jnp.float32) * 2.0
    noise_two = jax.random.normal(key_noise_two, (SNPS, INDIV), jnp.float32) * 2.0
    logit_one = jnp.where(first_allele, 2.5, -2.5) + noise_one
    logit_two = jnp.where(second_allele, 2.5, -2.5) + noise_two
    dosage = jax.nn.sigmoid(logit_one) + jax.nn.sigmoid(logit_two)
    return jnp.where(missing, -1.0, dosage).astype(jnp.float32)


def draw_relationship(key, part):
    key = jax.random.fold_in(key, 23)
    key_noise, key_scale = jax.random.split(key, 2)
    spread = 0.02 / math.sqrt(INDIV)
    near_length = 6.0
    far_length = 48.0
    log_spread = 0.35
    noise_field = jax.random.normal(key_noise, (INDIV, INDIV), jnp.float32) * spread
    symmetric = (noise_field + noise_field.T) * 0.70710678
    row_scale = jnp.exp(jax.random.uniform(key_scale, (INDIV,), jnp.float32, -log_spread, log_spread))
    row_index = lax.broadcasted_iota(jnp.int32, (INDIV, INDIV), 0)
    col_index = lax.broadcasted_iota(jnp.int32, (INDIV, INDIV), 1)
    distance = jnp.abs(row_index - col_index).astype(jnp.float32)
    kinship = 0.7 * jnp.exp(-distance / near_length) + 0.3 * jnp.exp(-distance / far_length)
    return (row_scale[:, None] * kinship * row_scale[None, :] + symmetric).astype(jnp.float32)


def setup_inputs(seed: int = 0) -> dict:
    arg_keys = jax.random.split(jax.random.key(seed), 3)
    genotypes = draw_genotypes(jax.random.fold_in(arg_keys[2], 71), 0)
    relationship = draw_relationship(jax.random.fold_in(arg_keys[2], 71), 0)
    return {"genotypes": genotypes, "relationship": relationship}


RIDGE = 0.25

def reference(genotypes, relationship):
    called = genotypes >= 0
    dosage = jnp.where(called, genotypes, 0.0).astype(jnp.float32)
    totals = jnp.sum(dosage, axis=1)
    counts = jnp.sum(called.astype(jnp.float32), axis=1)
    frequency = totals / (2.0 * counts)
    scale_total = jnp.sum(2.0 * frequency * (1.0 - frequency))
    centered = jnp.where(called, dosage - 2.0 * frequency[:, None], 0.0).astype(jnp.bfloat16)
    gram = lax.dot_general(centered.astype(jnp.float32), centered.astype(jnp.float32), (((0,), (0,)), ((), ())), preferred_element_type=jnp.float32)
    combined = relationship + gram / scale_total
    diag_index = jnp.arange(INDIV, dtype=jnp.int32)
    combined = combined.at[diag_index, diag_index].add(RIDGE)
    factor = jnp.linalg.cholesky(combined[:PANEL, :PANEL])
    panel = lax.linalg.triangular_solve(factor, combined[:, :PANEL], left_side=False, lower=True, transpose_a=True)
    updated = combined - jnp.dot(panel, panel.T, precision=lax.Precision.HIGHEST)
    return (updated, panel)
```

```python
import jax
import jax.numpy as jnp
from jax import lax
from jax.experimental import pallas as pl
from jax.experimental.pallas import tpu as pltpu
from jax.sharding import PartitionSpec as P

PANEL = 512
RIDGE = 0.25
X, Y, Z, C = 4, 4, 8, 2
IND = 160
SNP = 768
WIDTH = 2560
COPIES = 240

HIGH = lax.Precision.HIGHEST
MESH = pl.DeviceIdType.MESH
F32 = jnp.float32
BF16 = jnp.bfloat16


def dot_tn(a, b, precision=HIGH):
    return lax.dot_general(a, b, (((0,), (0,)), ((), ())), precision=precision, preferred_element_type=F32)


def dot_nn(a, b, precision=HIGH):
    return lax.dot_general(a, b, (((1,), (0,)), ((), ())), precision=precision, preferred_element_type=F32)


def dot_nt(a, b, precision=None):
    return lax.dot_general(a, b, (((1,), (1,)), ((), ())), precision=precision, preferred_element_type=F32)


def three(x):
    high = x.astype(BF16)
    rest = x - high.astype(F32)
    mid = rest.astype(BF16)
    low = (rest - mid.astype(F32)).astype(BF16)
    return high.astype(F32), mid.astype(F32), low.astype(F32)


def outer_eight(a, b):
    ah, am, al = three(a)
    bh, bm, bl = three(b)
    left = jnp.concatenate([ah, ah, am, ah, al, am], 0).astype(BF16)
    right = jnp.concatenate([bh, bm, bh, bl, bh, bm], 0).astype(BF16)
    return dot_tn(left, right, None)


def eliminate_eight(row, inv, step):
    sub = lax.broadcasted_iota(jnp.int32, (8, 128), 0)
    cols = [jnp.broadcast_to(row[:, 8 * step + k : 8 * step + k + 1], (8, 128)) for k in range(8)]
    for j in range(8):
        root = lax.rsqrt(cols[j][j : j + 1, :])
        mult = jnp.where(sub > j, cols[j] * root, 0.0)
        row_j = row[j : j + 1, :] * root
        inv_j = inv[j : j + 1, :] * root
        row = jnp.where(sub == j, row_j, row - mult * row_j)
        inv = jnp.where(sub == j, inv_j, inv - mult * inv_j)
        for k in range(j + 1, 8):
            cols[k] = cols[k] - mult * (cols[k][j : j + 1, :] * root)
    return row, inv


def factor_block(d_ref):
    for step in range(16):
        lo = 8 * step
        row, inv = eliminate_eight(d_ref[lo : lo + 8, 0:128], d_ref[lo : lo + 8, 128:256], step)
        d_ref[lo : lo + 8, 0:128] = row
        d_ref[lo : lo + 8, 128:256] = inv
        if step < 15:
            prod = outer_eight(row, jnp.concatenate([row, inv], 1))
            d_ref[lo + 8 : 128, :] = d_ref[lo + 8 : 128, :] - prod[lo + 8 : 128, :]


def cholesky_part(b, a_ref, x_ref, d_ref):
    i0 = lax.broadcasted_iota(jnp.int32, (128, 128), 0)
    i1 = lax.broadcasted_iota(jnp.int32, (128, 128), 1)
    lo, hi = 128 * b, 128 * b + 128
    d_ref[:, 0:128] = a_ref[lo:hi, lo:hi]
    d_ref[:, 128:256] = jnp.where(i0 == i1, 1.0, 0.0).astype(F32)
    factor_block(d_ref)
    xd = d_ref[:, 128:256]
    x_row = dot_nn(xd, x_ref[lo:hi, 0:hi])
    x_ref[lo:hi, 0:hi] = x_row
    if hi < PANEL:
        right = dot_nn(xd, a_ref[lo:hi, hi:PANEL])
        a_ref[hi:PANEL, hi:PANEL] = a_ref[hi:PANEL, hi:PANEL] - dot_tn(right, right)
        x_ref[hi:PANEL, 0:hi] = x_ref[hi:PANEL, 0:hi] - dot_tn(right, x_row)


def kernel(
    gen, rel, out, panel,
    sum_a, sum_b, scale_buf, rel_piece, own_rows, cols, top, top_rel,
    part_a, recv_a, a11, part_u, recv_u, a21, upper, amat, xmat, dmat, comb_t, wmat,
    send_sem, recv_sem,
):
    x = lax.axis_index("snp")
    r = lax.axis_index("rows")
    y, z, c = r // 16, (r // 2) % 8, r % 2
    k_own = 2 * z + c
    count = [0]
    unsent = []

    def device(xx, yy, zz, cc):
        return (xx, yy * 16 + zz * 2 + cc)

    def x_peer(d):
        return device((x + d) % X, y, z, c)

    def y_peer(d):
        return device(x, (y + d) % Y, z, c)

    def z_peer(d):
        return device(x, y, (z + d) % Z, c)

    sibling = device(x, y, z, 1 - c)
    mirror = device(y, x, z, c)

    def slots(n):
        first = count[0]
        count[0] += n
        return first

    def describe(src, dst, to, slot):
        return pltpu.make_async_remote_copy(
            src_ref=src, dst_ref=dst, send_sem=send_sem.at[slot], recv_sem=recv_sem.at[slot],
            device_id=to, device_id_type=MESH,
        )

    def send(src, dst, to):
        copy = describe(src, dst, to, slots(1))
        copy.start()
        unsent.append((None, copy))
        return copy

    def send_if(cond, src, dst, to):
        copy = describe(src, dst, to, slots(1))
        pl.when(cond)(copy.start)
        unsent.append((cond, copy))
        return copy

    def arrive(copies):
        for copy in copies:
            copy.wait_recv()

    barrier = pltpu.get_barrier_semaphore()
    greeted = [x_peer(d) for d in range(1, X)]
    greeted += [device(x, (y + d) % Y, z, (c + e) % C) for d in range(Y) for e in range(C) if d or e]
    greeted += [z_peer(d) for d in range(1, Z)]
    for to in greeted:
        pl.semaphore_signal(barrier, inc=1, device_id=to, device_id_type=MESH)

    @pl.when(x != y)
    def _():
        pl.semaphore_signal(barrier, inc=1, device_id=mirror, device_id_type=MESH)
        pl.semaphore_wait(barrier, len(greeted) + 1)

    @pl.when(x == y)
    def _():
        pl.semaphore_wait(barrier, len(greeted))

    rel_copies = []
    rel_slot = slots(1)
    rel_send = slots(3)
    for d in range(1, X):
        copy = pltpu.make_async_remote_copy(
            src_ref=rel.at[:, 128 * d : 128 * d + 128], dst_ref=rel_piece,
            send_sem=send_sem.at[rel_send + d - 1], recv_sem=recv_sem.at[rel_slot],
            device_id=device(d, y, z, c), device_id_type=MESH,
        )
        rel_copies.append(copy)

    @pl.when(x == 0)
    def _():
        for copy in rel_copies:
            copy.start()
        rel_piece[...] = rel[:, 0:128]

    for copy in rel_copies:
        unsent.append((x == 0, copy))

    values = gen[...]
    called = values >= 0
    dosage = jnp.where(called, values, 0.0)
    sums = jnp.concatenate(
        [jnp.sum(dosage, axis=0, keepdims=True), jnp.sum(called.astype(F32), axis=0, keepdims=True)], 0
    )
    yc = 2 * y + c
    sum_a[yc] = sums
    copies = [
        send(sum_a.at[yc], sum_a.at[yc], device(x, (y + d) % Y, z, (c + e) % C))
        for d in range(Y) for e in range(C) if d or e
    ]
    arrive(copies)
    sum_b[z] = jnp.sum(sum_a[...], axis=0)
    copies = [send(sum_b.at[z], sum_b.at[z], z_peer(d)) for d in range(1, Z)]
    arrive(copies)
    both = jnp.sum(sum_b[...], axis=0)
    frequency = both[0:1, :] / (2.0 * both[1:2, :])
    scale_part = jnp.sum(2.0 * frequency * (1.0 - frequency))
    scale_buf[x] = jnp.full((8, 128), scale_part, F32)
    scale_copies = [send(scale_buf.at[x], scale_buf.at[x], x_peer(d)) for d in range(1, X)]
    own_rows[x] = jnp.where(called, dosage - 2.0 * frequency, 0.0).astype(BF16)

    @pl.when(x != 0)
    def _():
        rel_copies[0].wait_recv()

    def top_at(k, q):
        rows = pl.ds(pl.multiple_of(k * IND + 80 * (q // 2), 16), 80)
        lanes = pl.ds(pl.multiple_of(384 * (q % 2), 128), 384)
        return top.at[rows, lanes]

    def top_rel_at(k, q):
        return top_rel.at[pl.ds(pl.multiple_of(k * IND + 40 * q, 8), 40)]

    first_slot = slots(2)
    source = jnp.logical_and(y == 0, z < 2)
    to_send = []
    for d in range(1, Y):
        rows, lanes = pl.ds(80 * (d // 2), 80), pl.ds(384 * (d % 2), 384)
        send_slot = slots(2)
        for i, (src, dst) in enumerate((
            (own_rows.at[x, rows, lanes], top_at(k_own, d)),
            (rel_piece.at[pl.ds(40 * d, 40)], top_rel_at(k_own, d)),
        )):
            to_send.append(pltpu.make_async_remote_copy(
                src_ref=src, dst_ref=dst, send_sem=send_sem.at[send_slot + i], recv_sem=recv_sem.at[first_slot + i],
                device_id=device(x, d, z, c), device_id_type=MESH,
            ))

    @pl.when(source)
    def _():
        for copy in to_send:
            copy.start()
        top[pl.ds(pl.multiple_of(k_own * IND, 16), 80), 0:384] = own_rows[x, 0:80, 0:384]
        top_rel[pl.ds(pl.multiple_of(k_own * IND, 8), 40)] = rel_piece[0:40]

    for copy in to_send:
        unsent.append((source, copy))

    def col_at(a, k, part):
        return cols.at[a, pl.ds(pl.multiple_of(k * IND, 16), IND), pl.ds(384 * part, 384)]

    def up_at(a, k, part):
        return upper.at[a, pl.ds(pl.multiple_of(k * IND + 80 * part, 8), 80)]

    own_slice = pl.ds(pl.multiple_of(k_own * IND, 16), IND)
    swap = send_if(x != y, own_rows.at[x], cols.at[x, own_slice], mirror)

    @pl.when(x == y)
    def _():
        cols[x, own_slice] = own_rows[x]

    row_copies = [send(own_rows.at[x], own_rows.at[x], x_peer(d)) for d in range(1, X)]

    @pl.when(jnp.logical_and(y != 0, z < 2))
    def _():
        for copy in to_send[:2]:
            copy.wait_recv()

    z_slot = slots(4)
    z_copies = []
    for d in range(1, Z):
        send_slot = slots(2)
        for i, ref in enumerate((top_at(k_own, y), top_rel_at(k_own, y))):
            z_copies.append(pltpu.make_async_remote_copy(
                src_ref=ref, dst_ref=ref, send_sem=send_sem.at[send_slot + i],
                recv_sem=recv_sem.at[z_slot + 2 * (z % 2) + i], device_id=z_peer(d), device_id_type=MESH,
            ))

    @pl.when(z < 2)
    def _():
        for copy in z_copies:
            copy.start()

    for copy in z_copies:
        unsent.append((z < 2, copy))

    def plane_gather(at):
        every = slice(None)
        across = [send(at(y, k_own, 0), at(y, k_own, 0), y_peer(d)) for d in range(1, Y)]

        def ring(k_plus, k_minus, a, part, plus, minus):
            made = []
            if plus:
                made.append(send(at(a, k_plus, part), at(a, k_plus, part), z_peer(1)))
            if minus:
                made.append(send(at(a, k_minus, part), at(a, k_minus, part), z_peer(Z - 1)))
            return made

        ring_two = ring(k_own, k_own, y, 1, True, True)
        spread = [send(at(y, k_own, 1), at(y, k_own, 1), y_peer(d)) for d in range(1, Y)]
        yield
        arrive(across)
        ring_one = ring(k_own, k_own, every, 0, True, True)
        passed = [send(at(every, k_own, 0), at(every, k_own, 0), sibling)]
        spread_ks = [k_own]
        yield
        for t in range(1, 5):
            k_minus = 2 * ((z + t) % Z) + c
            k_plus = 2 * ((z + Z - t) % Z) + c
            ks = [k_plus, k_minus] if t < 4 else [k_plus]
            arrive(ring_two)
            if t < 4:
                ring_two = ring(k_plus, k_minus, y, 1, True, t < 3)
            later = [send(at(y, k, 1), at(y, k, 1), y_peer(d)) for k in ks for d in range(1, Y)]
            arrive(ring_one)
            if t < 4:
                ring_one = ring(k_plus, k_minus, every, 0, True, t < 3)
            passed += [send(at(every, k, 0), at(every, k, 0), sibling) for k in ks]
            arrive(spread)
            passed += [send(at(every, k, 1), at(every, k, 1), sibling) for k in spread_ks]
            spread, spread_ks = later, ks
            yield
        arrive(spread)
        passed += [send(at(every, k, 1), at(every, k, 1), sibling) for k in spread_ks]
        yield
        arrive(passed)
        yield

    @pl.when(x != y)
    def _():
        swap.wait_recv()

    gather = plane_gather(col_at)
    next(gather)

    for zs in range(2):
        @pl.when(z != zs)
        def _(zs=zs):
            for i, ref in enumerate((top_at(2 * zs + c, y), top_rel_at(2 * zs + c, y))):
                describe(ref, ref, z_peer(1), z_slot + 2 * zs + i).wait_recv()

    copies = [
        send(ref, ref, y_peer(d))
        for d in range(1, Y) for zs in range(2) for ref in (top_at(2 * zs + c, y), top_rel_at(2 * zs + c, y))
    ]
    next(gather)
    arrive(copies)
    whole = [pl.ds(pl.multiple_of((2 * zs + c) * IND, 16), IND) for zs in range(2)]
    copies = [send(ref.at[s], ref.at[s], sibling) for s in whole for ref in (top, top_rel)]
    arrive(copies)

    for xx in range(X):
        part_a[xx] = dot_nt(top[0:PANEL, :], top[128 * xx : 128 * xx + 128, :])
        part_u[xx] = dot_nt(own_rows[x], top[128 * xx : 128 * xx + 128, :])
    half = pl.ds(pl.multiple_of(256 * c, 8), 256)
    a_copies = [send(part_a.at[(x + d) % X, half], recv_a.at[d - 1], x_peer(d)) for d in range(1, X)]
    u_copies = [send(part_u.at[(x + d) % X], recv_u.at[d - 1], x_peer(d)) for d in range(1, X)]
    arrive(scale_copies)
    scale = 1.0 / (scale_buf[0] + scale_buf[1] + scale_buf[2] + scale_buf[3])[0:1, 0:1]

    next(gather)
    arrive(a_copies)
    lane = 128 * x + lax.broadcasted_iota(jnp.int32, (256, 128), 1)
    row = 256 * c + lax.broadcasted_iota(jnp.int32, (256, 128), 0)
    total = part_a[x, half] + recv_a[0] + recv_a[1] + recv_a[2]
    a11[x, half] = top_rel[half] + total * scale + jnp.where(lane == row, RIDGE, 0.0)
    a_copies = [send(a11.at[x, half], a11.at[x, half], x_peer(d)) for d in range(1, X)]
    arrive(u_copies)
    lane = 128 * x + lax.broadcasted_iota(jnp.int32, (IND, 128), 1)
    row = IND * r + lax.broadcasted_iota(jnp.int32, (IND, 128), 0)
    total = part_u[x] + recv_u[0] + recv_u[1] + recv_u[2]
    mine = rel_piece[...] + total * scale + jnp.where(lane == row, RIDGE, 0.0)
    a21[x] = mine
    u_swap = send_if(x != y, a21.at[x], upper.at[x, own_slice], mirror)

    @pl.when(x == y)
    def _():
        upper[x, own_slice] = mine

    u_copies = [send(a21.at[x], a21.at[x], x_peer(d)) for d in range(1, X)]
    arrive(a_copies)
    a_copy = send(a11.at[:, half], a11.at[:, half], sibling)
    next(gather)
    a_copy.wait_recv()
    for xx in range(X):
        amat[:, 128 * xx : 128 * xx + 128] = a11[xx]
    i0 = lax.broadcasted_iota(jnp.int32, (PANEL, PANEL), 0)
    i1 = lax.broadcasted_iota(jnp.int32, (PANEL, PANEL), 1)
    xmat[...] = jnp.where(i0 == i1, 1.0, 0.0).astype(F32)
    cholesky_part(0, amat, xmat, dmat)
    next(gather)
    cholesky_part(1, amat, xmat, dmat)
    next(gather)

    @pl.when(x != y)
    def _():
        u_swap.wait_recv()

    u_gather = plane_gather(up_at)
    next(u_gather)
    next(gather)
    cholesky_part(2, amat, xmat, dmat)
    next(u_gather)
    next(gather)
    next(u_gather)
    cholesky_part(3, amat, xmat, dmat)
    arrive(u_copies)
    own = jnp.concatenate([a21[0], a21[1], a21[2], a21[3]], 1)
    own_panel = dot_nt(own, xmat[...], HIGH)
    panel[...] = own_panel
    wmat[...] = dot_nn(own_panel, xmat[...])
    next(u_gather)

    arrive(row_copies)

    def gram_part(i, carry):
        rows = pl.ds(pl.multiple_of(i * 256, 16), 256)
        total = dot_nt(cols[0, rows], own_rows[0])
        for a in range(1, X):
            total = total + dot_nt(cols[a, rows], own_rows[a])
        comb_t[rows, :] = total * scale
        return carry

    lax.fori_loop(0, 5, gram_part, 0)
    next(u_gather)
    lax.fori_loop(5, 10, gram_part, 0)
    next(u_gather)
    next(u_gather)
    next(u_gather)

    def last_part(i, carry):
        rows = pl.ds(pl.multiple_of(i * 256, 16), 256)
        up = jnp.concatenate([upper[0, rows], upper[1, rows], upper[2, rows], upper[3, rows]], 1)
        comb_t[rows, :] = comb_t[rows, :] - dot_nt(up, wmat[...], HIGH)
        return carry

    lax.fori_loop(0, 10, last_part, 0)
    for i in range(WIDTH // 128):
        lanes = slice(128 * i, 128 * i + 128)
        lane = WIDTH * x + 128 * i + lax.broadcasted_iota(jnp.int32, (IND, 128), 1)
        out[:, lanes] = rel[:, lanes] + comb_t[lanes, :].T + jnp.where(lane == row, RIDGE, 0.0)

    for cond, copy in unsent:
        if cond is None:
            copy.wait_send()
        else:
            pl.when(cond)(copy.wait_send)
    assert count[0] <= COPIES, count[0]


def per_device(genotypes, relationship):
    vmem = pl.BlockSpec(memory_space=pltpu.VMEM)
    return pl.pallas_call(
        kernel,
        out_shape=(
            jax.ShapeDtypeStruct((IND, WIDTH), F32),
            jax.ShapeDtypeStruct((IND, PANEL), F32),
        ),
        in_specs=[vmem, vmem],
        out_specs=(vmem, vmem),
        scratch_shapes=[
            pltpu.VMEM((8, 2, SNP), F32),
            pltpu.VMEM((8, 2, SNP), F32),
            pltpu.VMEM((X, 8, 128), F32),
            pltpu.VMEM((IND, 128), F32),
            pltpu.VMEM((X, IND, SNP), BF16),
            pltpu.VMEM((X, WIDTH, SNP), BF16),
            pltpu.VMEM((640, SNP), BF16),
            pltpu.VMEM((640, 128), F32),
            pltpu.VMEM((X, PANEL, 128), F32),
            pltpu.VMEM((3, 256, 128), F32),
            pltpu.VMEM((X, PANEL, 128), F32),
            pltpu.VMEM((X, IND, 128), F32),
            pltpu.VMEM((3, IND, 128), F32),
            pltpu.VMEM((X, IND, 128), F32),
            pltpu.VMEM((X, WIDTH, 128), F32),
            pltpu.VMEM((PANEL, PANEL), F32),
            pltpu.VMEM((PANEL, PANEL), F32),
            pltpu.VMEM((128, 256), F32),
            pltpu.VMEM((WIDTH, IND), F32),
            pltpu.VMEM((IND, PANEL), F32),
            pltpu.SemaphoreType.DMA((COPIES,)),
            pltpu.SemaphoreType.DMA((COPIES,)),
        ],
        compiler_params=pltpu.CompilerParams(
            collective_id=0, has_side_effects=True, vmem_limit_bytes=56 * 1024 * 1024
        ),
        name="update",
    )(genotypes.T, relationship)


def solution(mesh):
    return jax.shard_map(
        per_device,
        mesh=mesh,
        in_specs=(P("snp", "rows"), P("rows", "snp")),
        out_specs=(P("rows", "snp"), P("rows", None)),
        check_vma=False,
    )
```

```python
import jax
import jax.numpy as jnp
from jax import lax
from jax.experimental import pallas as pl
from jax.experimental.pallas import tpu as pltpu
from jax.sharding import PartitionSpec as P

PANEL = 512
RIDGE = 0.25
X, Y, Z, C = 4, 4, 8, 2
IND = 160
SNP = 768
WIDTH = 2560
COPIES = 320

HIGH = lax.Precision.HIGHEST
MESH = pl.DeviceIdType.MESH
F32 = jnp.float32
BF16 = jnp.bfloat16


def dot_tn(a, b, precision=HIGH):
    return lax.dot_general(a, b, (((0,), (0,)), ((), ())), precision=precision, preferred_element_type=F32)


def dot_nn(a, b, precision=HIGH):
    return lax.dot_general(a, b, (((1,), (0,)), ((), ())), precision=precision, preferred_element_type=F32)


def dot_nt(a, b, precision=None):
    return lax.dot_general(a, b, (((1,), (1,)), ((), ())), precision=precision, preferred_element_type=F32)


def three(x):
    high = x.astype(BF16)
    rest = x - high.astype(F32)
    mid = rest.astype(BF16)
    low = (rest - mid.astype(F32)).astype(BF16)
    return high.astype(F32), mid.astype(F32), low.astype(F32)


def outer_eight(a, b):
    ah, am, al = three(a)
    bh, bm, bl = three(b)
    left = jnp.concatenate([ah, ah, am, ah, al, am], 0).astype(BF16)
    right = jnp.concatenate([bh, bm, bh, bl, bh, bm], 0).astype(BF16)
    return dot_tn(left, right, None)


def eliminate_eight(row, inv, step):
    sub = lax.broadcasted_iota(jnp.int32, (8, 128), 0)
    cols = [jnp.broadcast_to(row[:, 8 * step + k : 8 * step + k + 1], (8, 128)) for k in range(8)]
    for j in range(8):
        root = lax.rsqrt(cols[j][j : j + 1, :])
        mult = jnp.where(sub > j, cols[j] * root, 0.0)
        row_j = row[j : j + 1, :] * root
        inv_j = inv[j : j + 1, :] * root
        row = jnp.where(sub == j, row_j, row - mult * row_j)
        inv = jnp.where(sub == j, inv_j, inv - mult * inv_j)
        for k in range(j + 1, 8):
            cols[k] = cols[k] - mult * (cols[k][j : j + 1, :] * root)
    return row, inv


def factor_steps(d_ref, first, last):
    for step in range(first, last):
        lo = 8 * step
        row, inv = eliminate_eight(d_ref[lo : lo + 8, 0:128], d_ref[lo : lo + 8, 128:256], step)
        d_ref[lo : lo + 8, 0:128] = row
        d_ref[lo : lo + 8, 128:256] = inv
        if step < 15:
            prod = outer_eight(row, jnp.concatenate([row, inv], 1))
            d_ref[lo + 8 : 128, :] = d_ref[lo + 8 : 128, :] - prod[lo + 8 : 128, :]


def cholesky_first(b, a_ref, d_ref):
    i0 = lax.broadcasted_iota(jnp.int32, (128, 128), 0)
    i1 = lax.broadcasted_iota(jnp.int32, (128, 128), 1)
    lo, hi = 128 * b, 128 * b + 128
    d_ref[:, 0:128] = a_ref[lo:hi, lo:hi]
    d_ref[:, 128:256] = jnp.where(i0 == i1, 1.0, 0.0).astype(F32)
    factor_steps(d_ref, 0, 8)


def cholesky_second(b, a_ref, x_ref, d_ref):
    lo, hi = 128 * b, 128 * b + 128
    factor_steps(d_ref, 8, 16)
    xd = d_ref[:, 128:256]
    x_row = dot_nn(xd, x_ref[lo:hi, 0:hi])
    x_ref[lo:hi, 0:hi] = x_row
    if hi < PANEL:
        right = dot_nn(xd, a_ref[lo:hi, hi:PANEL])
        a_ref[hi:PANEL, hi:PANEL] = a_ref[hi:PANEL, hi:PANEL] - dot_tn(right, right)
        x_ref[hi:PANEL, 0:hi] = x_ref[hi:PANEL, 0:hi] - dot_tn(right, x_row)


def kernel(
    gen, rel, out, panel,
    sum_a, sum_b, scale_buf, rel_piece, own_rows, cols, top, top_a,
    early, part_e, recv_e, piece, a11, part_u, recv_u, a21, upper, amat, xmat, dmat, comb_t,
    local_sem, send_sem, recv_sem,
):
    x = lax.axis_index("snp")
    r = lax.axis_index("rows")
    y, z, c = r // 16, (r // 2) % 8, r % 2
    k_own = 2 * z + c
    count = [0]
    unsent = []

    def device(xx, yy, zz, cc):
        return (xx, yy * 16 + zz * 2 + cc)

    def x_peer(d):
        return device((x + d) % X, y, z, c)

    def y_peer(d):
        return device(x, (y + d) % Y, z, c)

    def z_peer(d):
        return device(x, y, (z + d) % Z, c)

    sibling = device(x, y, z, 1 - c)
    mirror = device(y, x, z, c)

    def slots(n):
        first = count[0]
        count[0] += n
        return first

    def describe(src, dst, to, slot):
        return pltpu.make_async_remote_copy(
            src_ref=src, dst_ref=dst, send_sem=send_sem.at[slot], recv_sem=recv_sem.at[slot],
            device_id=to, device_id_type=MESH,
        )

    def send(src, dst, to):
        copy = describe(src, dst, to, slots(1))
        copy.start()
        unsent.append((None, copy))
        return copy

    def send_if(cond, src, dst, to):
        copy = describe(src, dst, to, slots(1))
        pl.when(cond)(copy.start)
        unsent.append((cond, copy))
        return copy

    def arrive(copies):
        for copy in copies:
            copy.wait_recv()

    barrier = pltpu.get_barrier_semaphore()
    greeted = [x_peer(d) for d in range(1, X)]
    greeted += [device(x, (y + d) % Y, z, (c + e) % C) for d in range(Y) for e in range(C) if d or e]
    greeted += [z_peer(d) for d in range(1, Z)]
    for to in greeted:
        pl.semaphore_signal(barrier, inc=1, device_id=to, device_id_type=MESH)

    @pl.when(x != y)
    def _():
        pl.semaphore_signal(barrier, inc=1, device_id=mirror, device_id_type=MESH)

    values = gen[...]
    called = values >= 0
    dosage = jnp.where(called, values, 0.0)
    sums = jnp.concatenate(
        [jnp.sum(dosage, axis=0, keepdims=True), jnp.sum(called.astype(F32), axis=0, keepdims=True)], 0
    )
    yc = 2 * y + c
    sum_a[yc] = sums

    @pl.when(x != y)
    def _():
        pl.semaphore_wait(barrier, len(greeted) + 1)

    @pl.when(x == y)
    def _():
        pl.semaphore_wait(barrier, len(greeted))

    rel_copies = []
    rel_slot = slots(1)
    rel_send = slots(3)
    for d in range(1, X):
        copy = pltpu.make_async_remote_copy(
            src_ref=rel.at[:, 128 * d : 128 * d + 128], dst_ref=rel_piece,
            send_sem=send_sem.at[rel_send + d - 1], recv_sem=recv_sem.at[rel_slot],
            device_id=device(d, y, z, c), device_id_type=MESH,
        )
        rel_copies.append(copy)

    @pl.when(x == 0)
    def _():
        for copy in rel_copies:
            copy.start()
        local = pltpu.make_async_copy(rel.at[:, 0:128], rel_piece, local_sem)
        local.start()
        local.wait()

    for copy in rel_copies:
        unsent.append((x == 0, copy))

    copies = [
        send(sum_a.at[yc], sum_a.at[yc], device(x, (y + d) % Y, z, (c + e) % C))
        for d in range(Y) for e in range(C) if d or e
    ]
    arrive(copies)
    sum_b[z] = jnp.sum(sum_a[...], axis=0)
    copies = [send(sum_b.at[z], sum_b.at[z], z_peer(d)) for d in range(1, Z)]
    arrive(copies)
    both = jnp.sum(sum_b[...], axis=0)
    frequency = both[0:1, :] / (2.0 * both[1:2, :])
    scale_part = jnp.sum(2.0 * frequency * (1.0 - frequency))
    scale_buf[x] = jnp.full((8, 128), scale_part, F32)
    scale_copies = [send(scale_buf.at[x], scale_buf.at[x], x_peer(d)) for d in range(1, X)]
    own_rows[x] = jnp.where(called, dosage - 2.0 * frequency, 0.0).astype(BF16)

    def wait_if(cond, copies):
        @pl.when(cond)
        def _():
            for copy in copies:
                copy.wait_recv()

    wait_if(x != 0, rel_copies[:1])
    source = jnp.logical_and(y == 0, z < 2)
    own_slice = pl.ds(pl.multiple_of(k_own * IND, 16), IND)

    class Broadcast:
        def __init__(self, block, at, whole):
            self.at, self.whole = at, whole
            slot, first = slots(1), slots(Y - 1)
            self.quarters = [
                pltpu.make_async_remote_copy(
                    src_ref=block(q), dst_ref=at(k_own, q), send_sem=send_sem.at[first + q - 1],
                    recv_sem=recv_sem.at[slot], device_id=device(x, q, z, c), device_id_type=MESH,
                )
                for q in range(1, Y)
            ]

            @pl.when(source)
            def _():
                for copy in self.quarters:
                    copy.start()
                at(k_own, 0)[...] = block(0)[...]

            for copy in self.quarters:
                unsent.append((source, copy))

        def along_z(self):
            wait_if(jnp.logical_and(y != 0, z < 2), self.quarters[:1])
            self.slot, first = slots(2), slots(Z - 1)
            ref = self.at(k_own, y)
            copies = [
                pltpu.make_async_remote_copy(
                    src_ref=ref, dst_ref=ref, send_sem=send_sem.at[first + d - 1],
                    recv_sem=recv_sem.at[self.slot + z % 2], device_id=z_peer(d), device_id_type=MESH,
                )
                for d in range(1, Z)
            ]

            @pl.when(z < 2)
            def _():
                for copy in copies:
                    copy.start()

            for copy in copies:
                unsent.append((z < 2, copy))

        def along_y(self):
            refs = [self.at(2 * zs + c, y) for zs in range(2)]
            for zs in range(2):
                wait_if(z != zs, [describe(refs[zs], refs[zs], z_peer(1), self.slot + zs)])
            self.copies = [send(ref, ref, y_peer(d)) for d in range(1, Y) for ref in refs]

        def to_sibling(self):
            arrive(self.copies)
            refs = [self.whole(2 * zs + c) for zs in range(2)]
            self.copies = [send(ref, ref, sibling) for ref in refs]

        def finish(self):
            arrive(self.copies)

    def quarter(first, q):
        rows = pl.ds(pl.multiple_of(first + 80 * (q // 2), 16), 80)
        return rows, pl.ds(pl.multiple_of(384 * (q % 2), 128), 384)

    z_mate = device(x, y, z + 1 - 2 * (z % 2), c)
    early_copies = [send_if(source, own_rows.at[x], early.at[own_slice], z_mate)]
    top_cast = Broadcast(
        lambda q: own_rows.at[(x,) + quarter(0, q)],
        lambda k, q: top.at[quarter(k * IND, q)],
        lambda k: top.at[pl.ds(pl.multiple_of(k * IND, 16), IND)],
    )
    swap = send_if(x != y, own_rows.at[x], cols.at[x, own_slice], mirror)

    @pl.when(x == y)
    def _():
        cols[x, own_slice] = own_rows[x]

    @pl.when(source)
    def _():
        early[own_slice] = own_rows[x]

    top_cast.along_z()
    wait_if(source, early_copies)
    early_copies = []
    for zs in range(2):
        ref = early.at[pl.ds(pl.multiple_of((2 * zs + c) * IND, 16), IND)]
        early_copies.append(send_if(source, ref, ref, sibling))
    wait_if(source, early_copies)

    @pl.when(source)
    def _():
        for xx in range(X):
            part_e[xx] = dot_nt(own_rows[x], early[128 * xx : 128 * xx + 128, :])

    early_copies = [send_if(source, part_e.at[(x + d) % X], recv_e.at[d - 1], x_peer(d)) for d in range(1, X)]
    arrive(scale_copies)
    scale = 1.0 / (scale_buf[0] + scale_buf[1] + scale_buf[2] + scale_buf[3])[0:1, 0:1]

    def add_up(part, recv):
        lane = 128 * x + lax.broadcasted_iota(jnp.int32, (IND, 128), 1)
        row = IND * r + lax.broadcasted_iota(jnp.int32, (IND, 128), 0)
        total = part[x] + recv[0] + recv[1] + recv[2]
        return rel_piece[...] + total * scale + jnp.where(lane == row, RIDGE, 0.0)

    def part_rows(k, part, half):
        first, size = (0, 64) if part == 0 else (64, 96)
        if half is not None:
            first, size = first + size // 2 * half, size // 2
        return pl.ds(pl.multiple_of(k * IND + first, 16), size)

    def col_at(a, k, part, half=None):
        return cols.at[a, part_rows(k, part, half)]

    def up_at(a, k, part, half=None):
        return upper.at[a, part_rows(k, part, half)]

    class Gather:
        def __init__(self, at):
            self.at = at
            self.passed = {}
            self.across = [self.move(at(y, k_own, 0), y_peer(d)) for d in range(1, Y)]
            self.ring_two = [self.move(at(y, k_own, 1), z_peer(d)) for d in (1, Z - 1)]
            self.near = [(0, [k_own], self.fan([k_own]))]
            self.far = []

        def move(self, ref, to):
            return send(ref, ref, to)

        def fan(self, ks):
            return [self.move(self.at(y, k, 1), y_peer(d)) for k in ks for d in (1, Y - 1)]

        def at_distance(self, t):
            return 2 * ((z + Z - t) % Z) + c, 2 * ((z + t) % Z) + c

        def two(self, t):
            arrive(self.ring_two)
            plus, minus = self.at_distance(t)
            if t < 3:
                self.ring_two = [self.move(self.at(y, plus, 1), z_peer(1)), self.move(self.at(y, minus, 1), z_peer(Z - 1))]
            elif t == 3:
                self.ring_two = [
                    self.move(self.at(y, plus, 1, 0), z_peer(1)), self.move(self.at(y, minus, 1, 1), z_peer(Z - 1))
                ]
            ks = [plus, minus] if t < 4 else [plus]
            self.near.append((t, ks, self.fan(ks)))

        def one(self, t):
            if t == 0:
                arrive(self.across)
            plus, minus = self.at_distance(t)
            low, high = slice(0, 2), slice(2, 4)
            after = []
            for i, some in enumerate((low, high)):
                if t > 0:
                    arrive(self.ring_one[2 * i : 2 * i + 2])
                if t < 3:
                    after += [self.move(self.at(some, plus, 0), z_peer(1)), self.move(self.at(some, minus, 0), z_peer(Z - 1))]
                elif t == 3 and i == 0:
                    after.append(self.move(self.at(low, plus, 0), z_peer(1)))
                elif t == 3:
                    after.append(self.move(self.at(high, minus, 0), z_peer(Z - 1)))
            self.ring_one = after
            self.hand_on([plus, minus] if 0 < t < 4 else [plus], t, 0)

        def hop(self):
            t, ks, copies = self.near.pop(0)
            arrive(copies)
            made = []
            for k in ks:
                made.append(self.move(self.at((y + Y - 1) % Y, k, 1, 0), y_peer(1)))
                made.append(self.move(self.at((y + 1) % Y, k, 1, 1), y_peer(Y - 1)))
            self.far.append((t, ks, made))

        def pass_two(self):
            t, ks, copies = self.far.pop(0)
            arrive(copies)
            self.hand_on(ks, t, 1)

        def hand_on(self, ks, t, part):
            made = [self.move(self.at(slice(None), k, part), sibling) for k in ks]
            self.passed.setdefault(t, []).extend(made)

        def complete(self, t):
            arrive(self.passed[t])

        def finish(self):
            while self.near:
                self.hop()
                if len(self.far) > 1:
                    self.pass_two()
            while self.far:
                self.pass_two()

    wait_if(x != y, [swap])
    gather = Gather(col_at)
    row_copies = [send(own_rows.at[x], own_rows.at[x], x_peer(d)) for d in range(1, X)]
    wait_if(source, early_copies)

    @pl.when(source)
    def _():
        piece[...] = add_up(part_e, recv_e)

    a_cast = Broadcast(
        lambda q: piece.at[pl.ds(40 * q, 40)],
        lambda k, q: top_a.at[pl.ds(pl.multiple_of(k * IND + 40 * q, 8), 40)],
        lambda k: top_a.at[pl.ds(pl.multiple_of(k * IND, 8), IND)],
    )
    a_cast.along_z()
    top_cast.along_y()
    gather.two(1)
    gather.one(0)
    a_cast.along_y()
    gather.two(2)
    gather.hop()
    a_cast.to_sibling()
    a_cast.finish()
    half = pl.ds(pl.multiple_of(256 * c, 8), 256)
    a11[x, half] = top_a[half]
    a_copies = [send(a11.at[x, half], a11.at[x, half], x_peer(d)) for d in range(1, X)]
    top_cast.to_sibling()
    gather.two(3)
    gather.hop()
    gather.pass_two()
    top_cast.finish()

    for xx in range(X):
        part_u[xx] = dot_nt(own_rows[x], top[128 * xx : 128 * xx + 128, :])
    u_copies = [send(part_u.at[(x + d) % X], recv_u.at[d - 1], x_peer(d)) for d in range(1, X)]
    gather.one(1)
    arrive(a_copies)
    a_copy = send(a11.at[:, half], a11.at[:, half], sibling)
    gather.two(4)
    gather.hop()
    gather.pass_two()
    a_copy.wait_recv()
    for xx in range(X):
        amat[:, 128 * xx : 128 * xx + 128] = a11[xx]
    i0 = lax.broadcasted_iota(jnp.int32, (PANEL, PANEL), 0)
    i1 = lax.broadcasted_iota(jnp.int32, (PANEL, PANEL), 1)
    xmat[...] = jnp.where(i0 == i1, 1.0, 0.0).astype(F32)
    arrive(u_copies)
    mine = add_up(part_u, recv_u)
    a21[x] = mine
    u_swap = send_if(x != y, a21.at[x], upper.at[x, own_slice], mirror)

    @pl.when(x == y)
    def _():
        upper[x, own_slice] = mine

    u_copies = [send(a21.at[x], a21.at[x], x_peer(d)) for d in range(1, X)]
    cholesky_first(0, amat, dmat)
    gather.one(2)
    gather.hop()
    gather.pass_two()
    wait_if(x != y, [u_swap])
    u_gather = Gather(up_at)
    cholesky_second(0, amat, xmat, dmat)
    gather.hop()
    gather.pass_two()
    u_gather.two(1)
    u_gather.one(0)
    cholesky_first(1, amat, dmat)
    gather.one(3)
    gather.pass_two()
    u_gather.two(2)
    u_gather.hop()
    cholesky_second(1, amat, xmat, dmat)
    u_gather.two(3)
    u_gather.hop()
    u_gather.one(1)
    cholesky_first(2, amat, dmat)
    gather.one(4)
    u_gather.pass_two()
    u_gather.two(4)
    u_gather.hop()
    arrive(row_copies)

    def chips(t):
        return [(z + Z - t) % Z, (z + t) % Z] if 0 < t < 4 else [(z + t) % Z]

    def gram_part(t):
        gather.complete(t)
        for chip in chips(t):
            rows = pl.ds(pl.multiple_of(chip * 320, 16), 320)
            total = dot_nt(cols[0, rows], own_rows[0])
            for a in range(1, X):
                total = total + dot_nt(cols[a, rows], own_rows[a])
            comb_t[rows, :] = total * scale

    gram_part(0)
    cholesky_second(2, amat, xmat, dmat)
    u_gather.one(2)
    u_gather.pass_two()
    u_gather.hop()
    gram_part(1)
    cholesky_first(3, amat, dmat)
    u_gather.one(3)
    u_gather.pass_two()
    u_gather.hop()
    gram_part(2)
    cholesky_second(3, amat, xmat, dmat)
    u_gather.one(4)
    u_gather.pass_two()
    gather.finish()
    u_gather.finish()
    arrive(u_copies)
    own = jnp.concatenate([a21[0], a21[1], a21[2], a21[3]], 1)
    own_panel = dot_nt(own, xmat[...], HIGH)
    panel[...] = own_panel
    weights = dot_nn(own_panel, xmat[...])
    w_high = weights.astype(BF16)
    w_low = (weights - w_high.astype(F32)).astype(BF16)
    gram_part(3)
    gram_part(4)
    for t in range(5):
        u_gather.complete(t)
        for chip in chips(t):
            rows = pl.ds(pl.multiple_of(chip * 320, 16), 320)
            up = jnp.concatenate([upper[0, rows], upper[1, rows], upper[2, rows], upper[3, rows]], 1)
            up_high = up.astype(BF16)
            up_low = (up - up_high.astype(F32)).astype(BF16)
            prod = dot_nt(up_low, w_high) + dot_nt(up_high, w_low) + dot_nt(up_high, w_high)
            comb_t[rows, :] = comb_t[rows, :] - prod
    for i in range(WIDTH // 128):
        lanes = slice(128 * i, 128 * i + 128)
        out[:, lanes] = comb_t[lanes, :].T

    for cond, copy in unsent:
        if cond is None:
            copy.wait_send()
        else:
            pl.when(cond)(copy.wait_send)
    assert count[0] <= COPIES, count[0]


def per_device(genotypes, relationship):
    vmem = pl.BlockSpec(memory_space=pltpu.VMEM)
    added, own_panel = pl.pallas_call(
        kernel,
        out_shape=(
            jax.ShapeDtypeStruct((IND, WIDTH), F32),
            jax.ShapeDtypeStruct((IND, PANEL), F32),
        ),
        in_specs=[vmem, pl.BlockSpec(memory_space=pl.ANY)],
        out_specs=(vmem, vmem),
        scratch_shapes=[
            pltpu.VMEM((8, 2, SNP), F32),
            pltpu.VMEM((8, 2, SNP), F32),
            pltpu.VMEM((X, 8, 128), F32),
            pltpu.VMEM((IND, 128), F32),
            pltpu.VMEM((X, IND, SNP), BF16),
            pltpu.VMEM((X, WIDTH, SNP), BF16),
            pltpu.VMEM((640, SNP), BF16),
            pltpu.VMEM((640, 128), F32),
            pltpu.VMEM((640, SNP), BF16),
            pltpu.VMEM((X, IND, 128), F32),
            pltpu.VMEM((3, IND, 128), F32),
            pltpu.VMEM((IND, 128), F32),
            pltpu.VMEM((X, PANEL, 128), F32),
            pltpu.VMEM((X, IND, 128), F32),
            pltpu.VMEM((3, IND, 128), F32),
            pltpu.VMEM((X, IND, 128), F32),
            pltpu.VMEM((X, WIDTH, 128), F32),
            pltpu.VMEM((PANEL, PANEL), F32),
            pltpu.VMEM((PANEL, PANEL), F32),
            pltpu.VMEM((128, 256), F32),
            pltpu.VMEM((WIDTH, IND), F32),
            pltpu.SemaphoreType.DMA,
            pltpu.SemaphoreType.DMA((COPIES,)),
            pltpu.SemaphoreType.DMA((COPIES,)),
        ],
        compiler_params=pltpu.CompilerParams(
            collective_id=0, has_side_effects=True, vmem_limit_bytes=56 * 1024 * 1024
        ),
        name="update",
    )(genotypes.T, relationship)
    row = IND * lax.axis_index("rows") + lax.broadcasted_iota(jnp.int32, (IND, WIDTH), 0)
    col = WIDTH * lax.axis_index("snp") + lax.broadcasted_iota(jnp.int32, (IND, WIDTH), 1)
    return relationship + added + jnp.where(row == col, RIDGE, 0.0), own_panel


def solution(mesh):
    return jax.shard_map(
        per_device,
        mesh=mesh,
        in_specs=(P("snp", "rows"), P("rows", "snp")),
        out_specs=(P("rows", "snp"), P("rows", None)),
        check_vma=False,
    )
```

```python
import jax
import jax.numpy as jnp
from jax import lax
from jax.experimental import pallas as pl
from jax.experimental.pallas import tpu as pltpu
from jax.sharding import PartitionSpec as P

PANEL = 512
RIDGE = 0.25
X, Y, Z, C = 4, 4, 8, 2
IND = 160
SNP = 768
WIDTH = 2560
COPIES = 320

HIGH = lax.Precision.HIGHEST
MESH = pl.DeviceIdType.MESH
F32 = jnp.float32
BF16 = jnp.bfloat16


def dot_tn(a, b, precision=HIGH):
    return lax.dot_general(a, b, (((0,), (0,)), ((), ())), precision=precision, preferred_element_type=F32)


def dot_nn(a, b, precision=HIGH):
    return lax.dot_general(a, b, (((1,), (0,)), ((), ())), precision=precision, preferred_element_type=F32)


def dot_nt(a, b, precision=None):
    return lax.dot_general(a, b, (((1,), (1,)), ((), ())), precision=precision, preferred_element_type=F32)


def three(x):
    high = x.astype(BF16)
    rest = x - high.astype(F32)
    mid = rest.astype(BF16)
    low = (rest - mid.astype(F32)).astype(BF16)
    return high.astype(F32), mid.astype(F32), low.astype(F32)


def outer_eight(a, b):
    ah, am, al = three(a)
    bh, bm, bl = three(b)
    left = jnp.concatenate([ah, ah, am, ah, al, am], 0).astype(BF16)
    right = jnp.concatenate([bh, bm, bh, bl, bh, bm], 0).astype(BF16)
    return dot_tn(left, right, None)


def eliminate_eight(row, inv, step):
    sub = lax.broadcasted_iota(jnp.int32, (8, 128), 0)
    cols = [jnp.broadcast_to(row[:, 8 * step + k : 8 * step + k + 1], (8, 128)) for k in range(8)]
    for j in range(8):
        root = lax.rsqrt(cols[j][j : j + 1, :])
        mult = jnp.where(sub > j, cols[j] * root, 0.0)
        row_j = row[j : j + 1, :] * root
        inv_j = inv[j : j + 1, :] * root
        row = jnp.where(sub == j, row_j, row - mult * row_j)
        inv = jnp.where(sub == j, inv_j, inv - mult * inv_j)
        for k in range(j + 1, 8):
            cols[k] = cols[k] - mult * (cols[k][j : j + 1, :] * root)
    return row, inv


def factor_steps(d_ref, first, last):
    for step in range(first, last):
        lo = 8 * step
        row, inv = eliminate_eight(d_ref[lo : lo + 8, 0:128], d_ref[lo : lo + 8, 128:256], step)
        d_ref[lo : lo + 8, 0:128] = row
        d_ref[lo : lo + 8, 128:256] = inv
        if step < 15:
            prod = outer_eight(row, jnp.concatenate([row, inv], 1))
            d_ref[lo + 8 : 128, :] = d_ref[lo + 8 : 128, :] - prod[lo + 8 : 128, :]


def cholesky_first(b, a_ref, d_ref):
    i0 = lax.broadcasted_iota(jnp.int32, (128, 128), 0)
    i1 = lax.broadcasted_iota(jnp.int32, (128, 128), 1)
    lo, hi = 128 * b, 128 * b + 128
    d_ref[:, 0:128] = a_ref[lo:hi, lo:hi]
    d_ref[:, 128:256] = jnp.where(i0 == i1, 1.0, 0.0).astype(F32)
    factor_steps(d_ref, 0, 8)


def cholesky_second(b, a_ref, x_ref, d_ref):
    lo, hi = 128 * b, 128 * b + 128
    factor_steps(d_ref, 8, 16)
    xd = d_ref[:, 128:256]
    x_row = dot_nn(xd, x_ref[lo:hi, 0:hi])
    x_ref[lo:hi, 0:hi] = x_row
    if hi < PANEL:
        right = dot_nn(xd, a_ref[lo:hi, hi:PANEL])
        a_ref[hi:PANEL, hi:PANEL] = a_ref[hi:PANEL, hi:PANEL] - dot_tn(right, right)
        x_ref[hi:PANEL, 0:hi] = x_ref[hi:PANEL, 0:hi] - dot_tn(right, x_row)


def kernel(
    gen, rel, out, panel,
    sum_a, sum_b, scale_buf, rel_piece, own_rows, cols, top, top_a,
    early, part_e, recv_e, piece, a11, part_u, recv_u, a21, upper, amat, xmat, dmat, comb_t,
    local_sem, send_sem, recv_sem,
):
    x = lax.axis_index("snp")
    r = lax.axis_index("rows")
    y, z, c = r // 16, (r // 2) % 8, r % 2
    k_own = 2 * z + c
    count = [0]
    unsent = []

    def device(xx, yy, zz, cc):
        return (xx, yy * 16 + zz * 2 + cc)

    def x_peer(d):
        return device((x + d) % X, y, z, c)

    def y_peer(d):
        return device(x, (y + d) % Y, z, c)

    def z_peer(d):
        return device(x, y, (z + d) % Z, c)

    sibling = device(x, y, z, 1 - c)
    mirror = device(y, x, z, c)

    def slots(n):
        first = count[0]
        count[0] += n
        return first

    def describe(src, dst, to, slot):
        return pltpu.make_async_remote_copy(
            src_ref=src, dst_ref=dst, send_sem=send_sem.at[slot], recv_sem=recv_sem.at[slot],
            device_id=to, device_id_type=MESH,
        )

    def send(src, dst, to):
        copy = describe(src, dst, to, slots(1))
        copy.start()
        unsent.append((None, copy))
        return copy

    def send_if(cond, src, dst, to):
        copy = describe(src, dst, to, slots(1))
        pl.when(cond)(copy.start)
        unsent.append((cond, copy))
        return copy

    def arrive(copies):
        for copy in copies:
            copy.wait_recv()

    barrier = pltpu.get_barrier_semaphore()
    greeted = [x_peer(d) for d in range(1, X)]
    greeted += [device(x, (y + d) % Y, z, (c + e) % C) for d in range(Y) for e in range(C) if d or e]
    greeted += [z_peer(d) for d in range(1, Z)]
    for to in greeted:
        pl.semaphore_signal(barrier, inc=1, device_id=to, device_id_type=MESH)

    @pl.when(x != y)
    def _():
        pl.semaphore_signal(barrier, inc=1, device_id=mirror, device_id_type=MESH)

    values = gen[...]
    called = values >= 0
    dosage = jnp.where(called, values, 0.0)
    sums = jnp.concatenate(
        [jnp.sum(dosage, axis=0, keepdims=True), jnp.sum(called.astype(F32), axis=0, keepdims=True)], 0
    )
    yc = 2 * y + c
    sum_a[yc] = sums

    @pl.when(x != y)
    def _():
        pl.semaphore_wait(barrier, len(greeted) + 1)

    @pl.when(x == y)
    def _():
        pl.semaphore_wait(barrier, len(greeted))

    rel_copies = []
    rel_slot = slots(1)
    rel_send = slots(3)
    for d in range(1, X):
        copy = pltpu.make_async_remote_copy(
            src_ref=rel.at[:, 128 * d : 128 * d + 128], dst_ref=rel_piece,
            send_sem=send_sem.at[rel_send + d - 1], recv_sem=recv_sem.at[rel_slot],
            device_id=device(d, y, z, c), device_id_type=MESH,
        )
        rel_copies.append(copy)

    @pl.when(x == 0)
    def _():
        for copy in rel_copies:
            copy.start()
        local = pltpu.make_async_copy(rel.at[:, 0:128], rel_piece, local_sem)
        local.start()
        local.wait()

    for copy in rel_copies:
        unsent.append((x == 0, copy))

    copies = [
        send(sum_a.at[yc], sum_a.at[yc], device(x, (y + d) % Y, z, (c + e) % C))
        for d in range(Y) for e in range(C) if d or e
    ]
    arrive(copies)
    sum_b[z] = jnp.sum(sum_a[...], axis=0)
    copies = [send(sum_b.at[z], sum_b.at[z], z_peer(d)) for d in range(1, Z)]
    arrive(copies)
    both = jnp.sum(sum_b[...], axis=0)
    frequency = both[0:1, :] / (2.0 * both[1:2, :])
    scale_part = jnp.sum(2.0 * frequency * (1.0 - frequency))
    scale_buf[x] = jnp.full((8, 128), scale_part, F32)
    scale_copies = [send(scale_buf.at[x], scale_buf.at[x], x_peer(d)) for d in range(1, X)]
    own_rows[x] = jnp.where(called, dosage - 2.0 * frequency, 0.0).astype(BF16)

    def wait_if(cond, copies):
        @pl.when(cond)
        def _():
            for copy in copies:
                copy.wait_recv()

    wait_if(x != 0, rel_copies[:1])
    source = jnp.logical_and(y == 0, z < 2)
    own_slice = pl.ds(pl.multiple_of(k_own * IND, 16), IND)

    class Broadcast:
        def __init__(self, block, at, whole):
            self.at, self.whole = at, whole
            slot, first = slots(1), slots(Y - 1)
            self.quarters = [
                pltpu.make_async_remote_copy(
                    src_ref=block(q), dst_ref=at(k_own, q), send_sem=send_sem.at[first + q - 1],
                    recv_sem=recv_sem.at[slot], device_id=device(x, q, z, c), device_id_type=MESH,
                )
                for q in range(1, Y)
            ]

            @pl.when(source)
            def _():
                for copy in self.quarters:
                    copy.start()
                at(k_own, 0)[...] = block(0)[...]

            for copy in self.quarters:
                unsent.append((source, copy))

        def along_z(self):
            wait_if(jnp.logical_and(y != 0, z < 2), self.quarters[:1])
            self.slot, first = slots(2), slots(Z - 1)
            ref = self.at(k_own, y)
            copies = [
                pltpu.make_async_remote_copy(
                    src_ref=ref, dst_ref=ref, send_sem=send_sem.at[first + d - 1],
                    recv_sem=recv_sem.at[self.slot + z % 2], device_id=z_peer(d), device_id_type=MESH,
                )
                for d in range(1, Z)
            ]

            @pl.when(z < 2)
            def _():
                for copy in copies:
                    copy.start()

            for copy in copies:
                unsent.append((z < 2, copy))

        def along_y(self):
            refs = [self.at(2 * zs + c, y) for zs in range(2)]
            for zs in range(2):
                wait_if(z != zs, [describe(refs[zs], refs[zs], z_peer(1), self.slot + zs)])
            self.copies = [send(ref, ref, y_peer(d)) for d in range(1, Y) for ref in refs]

        def to_sibling(self):
            arrive(self.copies)
            refs = [self.whole(2 * zs + c) for zs in range(2)]
            self.copies = [send(ref, ref, sibling) for ref in refs]

        def finish(self):
            arrive(self.copies)

    def quarter(first, q):
        rows = pl.ds(pl.multiple_of(first + 80 * (q // 2), 16), 80)
        return rows, pl.ds(pl.multiple_of(384 * (q % 2), 128), 384)

    z_mate = device(x, y, z + 1 - 2 * (z % 2), c)
    early_copies = [send_if(source, own_rows.at[x], early.at[own_slice], z_mate)]
    top_cast = Broadcast(
        lambda q: own_rows.at[(x,) + quarter(0, q)],
        lambda k, q: top.at[quarter(k * IND, q)],
        lambda k: top.at[pl.ds(pl.multiple_of(k * IND, 16), IND)],
    )
    swap = send_if(x != y, own_rows.at[x], cols.at[x, own_slice], mirror)

    @pl.when(x == y)
    def _():
        cols[x, own_slice] = own_rows[x]

    @pl.when(source)
    def _():
        early[own_slice] = own_rows[x]

    top_cast.along_z()
    wait_if(source, early_copies)
    early_copies = []
    for zs in range(2):
        ref = early.at[pl.ds(pl.multiple_of((2 * zs + c) * IND, 16), IND)]
        early_copies.append(send_if(source, ref, ref, sibling))
    wait_if(source, early_copies)

    @pl.when(source)
    def _():
        for xx in range(X):
            part_e[xx] = dot_nt(own_rows[x], early[128 * xx : 128 * xx + 128, :])

    early_copies = [send_if(source, part_e.at[(x + d) % X], recv_e.at[d - 1], x_peer(d)) for d in range(1, X)]
    arrive(scale_copies)
    scale = 1.0 / (scale_buf[0] + scale_buf[1] + scale_buf[2] + scale_buf[3])[0:1, 0:1]

    def add_up(part, recv):
        lane = 128 * x + lax.broadcasted_iota(jnp.int32, (IND, 128), 1)
        row = IND * r + lax.broadcasted_iota(jnp.int32, (IND, 128), 0)
        total = part[x] + recv[0] + recv[1] + recv[2]
        return rel_piece[...] + total * scale + jnp.where(lane == row, RIDGE, 0.0)

    def part_rows(k, part, half):
        first, size = (0, 64) if part == 0 else (64, 96)
        if half is not None:
            first, size = first + size // 2 * half, size // 2
        return pl.ds(pl.multiple_of(k * IND + first, 16), size)

    def col_at(a, k, part, half=None):
        return cols.at[a, part_rows(k, part, half)]

    def up_at(a, k, part, half=None):
        return upper.at[a, part_rows(k, part, half)]

    class Gather:
        def __init__(self, at):
            self.at = at
            self.passed = {}
            self.across = [self.move(at(y, k_own, 0), y_peer(d)) for d in range(1, Y)]
            self.ring_two = [self.move(at(y, k_own, 1), z_peer(d)) for d in (1, Z - 1)]
            self.near = [(0, [k_own], self.fan([k_own]))]
            self.far = []

        def move(self, ref, to):
            return send(ref, ref, to)

        def fan(self, ks):
            return [self.move(self.at(y, k, 1), y_peer(d)) for k in ks for d in (1, Y - 1)]

        def at_distance(self, t):
            return 2 * ((z + Z - t) % Z) + c, 2 * ((z + t) % Z) + c

        def two(self, t):
            arrive(self.ring_two)
            plus, minus = self.at_distance(t)
            if t < 3:
                self.ring_two = [self.move(self.at(y, plus, 1), z_peer(1)), self.move(self.at(y, minus, 1), z_peer(Z - 1))]
            elif t == 3:
                self.ring_two = [
                    self.move(self.at(y, plus, 1, 0), z_peer(1)), self.move(self.at(y, minus, 1, 1), z_peer(Z - 1))
                ]
            ks = [plus, minus] if t < 4 else [plus]
            self.near.append((t, ks, self.fan(ks)))

        def one(self, t):
            if t == 0:
                arrive(self.across)
            plus, minus = self.at_distance(t)
            low, high = slice(0, 2), slice(2, 4)
            after = []
            for i, some in enumerate((low, high)):
                if t > 0:
                    arrive(self.ring_one[2 * i : 2 * i + 2])
                if t < 3:
                    after += [self.move(self.at(some, plus, 0), z_peer(1)), self.move(self.at(some, minus, 0), z_peer(Z - 1))]
                elif t == 3 and i == 0:
                    after.append(self.move(self.at(low, plus, 0), z_peer(1)))
                elif t == 3:
                    after.append(self.move(self.at(high, minus, 0), z_peer(Z - 1)))
            self.ring_one = after
            self.hand_on([plus, minus] if 0 < t < 4 else [plus], t, 0)

        def hop(self):
            t, ks, copies = self.near.pop(0)
            arrive(copies)
            made = []
            for k in ks:
                made.append(self.move(self.at((y + Y - 1) % Y, k, 1, 0), y_peer(1)))
                made.append(self.move(self.at((y + 1) % Y, k, 1, 1), y_peer(Y - 1)))
            self.far.append((t, ks, made))

        def pass_two(self):
            t, ks, copies = self.far.pop(0)
            arrive(copies)
            self.hand_on(ks, t, 1)

        def hand_on(self, ks, t, part):
            made = [self.move(self.at(slice(None), k, part), sibling) for k in ks]
            self.passed.setdefault(t, []).extend(made)

        def complete(self, t):
            arrive(self.passed[t])

        def finish(self):
            while self.near:
                self.hop()
                if len(self.far) > 1:
                    self.pass_two()
            while self.far:
                self.pass_two()

    wait_if(x != y, [swap])
    gather = Gather(col_at)
    row_copies = [send(own_rows.at[x], own_rows.at[x], x_peer(d)) for d in range(1, X)]
    wait_if(source, early_copies)

    @pl.when(source)
    def _():
        piece[...] = add_up(part_e, recv_e)

    a_cast = Broadcast(
        lambda q: piece.at[pl.ds(40 * q, 40)],
        lambda k, q: top_a.at[pl.ds(pl.multiple_of(k * IND + 40 * q, 8), 40)],
        lambda k: top_a.at[pl.ds(pl.multiple_of(k * IND, 8), IND)],
    )
    a_cast.along_z()
    top_cast.along_y()
    gather.two(1)
    gather.one(0)
    top_cast.to_sibling()
    a_cast.along_y()
    gather.two(2)
    gather.hop()
    top_cast.finish()

    for xx in range(X):
        part_u[xx] = dot_nt(own_rows[x], top[128 * xx : 128 * xx + 128, :])
    u_copies = [send(part_u.at[(x + d) % X], recv_u.at[d - 1], x_peer(d)) for d in range(1, X)]
    a_cast.to_sibling()
    a_cast.finish()
    half = pl.ds(pl.multiple_of(256 * c, 8), 256)
    a11[x, half] = top_a[half]
    a_copies = [send(a11.at[x, half], a11.at[x, half], x_peer(d)) for d in range(1, X)]
    gather.two(3)
    gather.hop()
    arrive(u_copies)
    mine = add_up(part_u, recv_u)
    a21[x] = mine
    u_swap = send_if(x != y, a21.at[x], upper.at[x, own_slice], mirror)

    @pl.when(x == y)
    def _():
        upper[x, own_slice] = mine

    u_copies = [send(a21.at[x], a21.at[x], x_peer(d)) for d in range(1, X)]
    arrive(a_copies)
    a_copy = send(a11.at[:, half], a11.at[:, half], sibling)
    gather.one(1)
    gather.two(4)
    gather.hop()
    wait_if(x != y, [u_swap])
    u_gather = Gather(up_at)
    a_copy.wait_recv()
    for xx in range(X):
        amat[:, 128 * xx : 128 * xx + 128] = a11[xx]
    i0 = lax.broadcasted_iota(jnp.int32, (PANEL, PANEL), 0)
    i1 = lax.broadcasted_iota(jnp.int32, (PANEL, PANEL), 1)
    xmat[...] = jnp.where(i0 == i1, 1.0, 0.0).astype(F32)
    def chips(t):
        return [(z + Z - t) % Z, (z + t) % Z] if 0 < t < 4 else [(z + t) % Z]

    def gram_part(t):
        gather.complete(t)
        for chip in chips(t):
            rows = pl.ds(pl.multiple_of(chip * 320, 16), 320)
            total = dot_nt(cols[0, rows], own_rows[0])
            for a in range(1, X):
                total = total + dot_nt(cols[a, rows], own_rows[a])
            comb_t[rows, :] = total * scale

    cholesky_first(0, amat, dmat)
    gather.one(2)
    gather.hop()
    gather.pass_two()
    cholesky_second(0, amat, xmat, dmat)
    gather.hop()
    gather.pass_two()
    u_gather.two(1)
    u_gather.one(0)
    cholesky_first(1, amat, dmat)
    gather.one(3)
    gather.pass_two()
    u_gather.two(2)
    u_gather.hop()
    cholesky_second(1, amat, xmat, dmat)
    gather.pass_two()
    u_gather.two(3)
    u_gather.hop()
    u_gather.one(1)
    cholesky_first(2, amat, dmat)
    gather.one(4)
    gather.pass_two()
    u_gather.two(4)
    u_gather.hop()
    arrive(row_copies)
    gram_part(0)
    cholesky_second(2, amat, xmat, dmat)
    u_gather.one(2)
    u_gather.pass_two()
    u_gather.hop()
    gram_part(1)
    cholesky_first(3, amat, dmat)
    u_gather.one(3)
    u_gather.pass_two()
    u_gather.pass_two()
    u_gather.hop()
    gram_part(2)
    cholesky_second(3, amat, xmat, dmat)
    u_gather.one(4)
    u_gather.pass_two()
    gather.finish()
    u_gather.finish()
    arrive(u_copies)
    own = jnp.concatenate([a21[0], a21[1], a21[2], a21[3]], 1)
    own_panel = dot_nt(own, xmat[...], HIGH)
    panel[...] = own_panel
    weights = dot_nn(own_panel, xmat[...])
    w_high = weights.astype(BF16)
    w_low = (weights - w_high.astype(F32)).astype(BF16)
    gram_part(3)
    gram_part(4)
    for t in range(5):
        u_gather.complete(t)
        for chip in chips(t):
            rows = pl.ds(pl.multiple_of(chip * 320, 16), 320)
            up = jnp.concatenate([upper[0, rows], upper[1, rows], upper[2, rows], upper[3, rows]], 1)
            up_high = up.astype(BF16)
            up_low = (up - up_high.astype(F32)).astype(BF16)
            prod = dot_nt(up_low, w_high) + dot_nt(up_high, w_low) + dot_nt(up_high, w_high)
            comb_t[rows, :] = comb_t[rows, :] - prod
    for i in range(WIDTH // 128):
        lanes = slice(128 * i, 128 * i + 128)
        lane = WIDTH * x + 128 * i + lax.broadcasted_iota(jnp.int32, (IND, 128), 1)
        row = IND * r + lax.broadcasted_iota(jnp.int32, (IND, 128), 0)
        out[:, lanes] = comb_t[lanes, :].T + jnp.where(lane == row, RIDGE, 0.0)

    for cond, copy in unsent:
        if cond is None:
            copy.wait_send()
        else:
            pl.when(cond)(copy.wait_send)
    assert count[0] <= COPIES, count[0]


def per_device(genotypes, relationship):
    vmem = pl.BlockSpec(memory_space=pltpu.VMEM)
    added, own_panel = pl.pallas_call(
        kernel,
        out_shape=(
            jax.ShapeDtypeStruct((IND, WIDTH), F32),
            jax.ShapeDtypeStruct((IND, PANEL), F32),
        ),
        in_specs=[vmem, pl.BlockSpec(memory_space=pl.ANY)],
        out_specs=(vmem, vmem),
        scratch_shapes=[
            pltpu.VMEM((8, 2, SNP), F32),
            pltpu.VMEM((8, 2, SNP), F32),
            pltpu.VMEM((X, 8, 128), F32),
            pltpu.VMEM((IND, 128), F32),
            pltpu.VMEM((X, IND, SNP), BF16),
            pltpu.VMEM((X, WIDTH, SNP), BF16),
            pltpu.VMEM((640, SNP), BF16),
            pltpu.VMEM((640, 128), F32),
            pltpu.VMEM((640, SNP), BF16),
            pltpu.VMEM((X, IND, 128), F32),
            pltpu.VMEM((3, IND, 128), F32),
            pltpu.VMEM((IND, 128), F32),
            pltpu.VMEM((X, PANEL, 128), F32),
            pltpu.VMEM((X, IND, 128), F32),
            pltpu.VMEM((3, IND, 128), F32),
            pltpu.VMEM((X, IND, 128), F32),
            pltpu.VMEM((X, WIDTH, 128), F32),
            pltpu.VMEM((PANEL, PANEL), F32),
            pltpu.VMEM((PANEL, PANEL), F32),
            pltpu.VMEM((128, 256), F32),
            pltpu.VMEM((WIDTH, IND), F32),
            pltpu.SemaphoreType.DMA,
            pltpu.SemaphoreType.DMA((COPIES,)),
            pltpu.SemaphoreType.DMA((COPIES,)),
        ],
        compiler_params=pltpu.CompilerParams(
            collective_id=0, has_side_effects=True, vmem_limit_bytes=56 * 1024 * 1024
        ),
        name="update",
    )(genotypes.T, relationship)
    return relationship + added, own_panel


def solution(mesh):
    return jax.shard_map(
        per_device,
        mesh=mesh,
        in_specs=(P("snp", "rows"), P("rows", "snp")),
        out_specs=(P("rows", "snp"), P("rows", None)),
        check_vma=False,
    )
```
